512 devices in a mesh: row: 32 (over y, z_hi, core), col: 16 (over x, z_lo).
Axes of the slice: x: 4, y: 4, z: 16 (z_hi: 4, z_lo: 4; z = z_hi * 4 + z_lo), core: 2. Of those that a mesh axis runs over, the one named last changes fastest.
Arguments:
- node_latents: bfloat16 [65536, 512], P(('row', 'col')), may hold values from -6 to 6
- fine_edges: bfloat16 [524288, 512], P(('row', 'col')), may hold values from -6 to 6
- fine_senders: int32 [524288], P(('row', 'col')), may hold values from 0 to 767, as said below
- degrees: int32 [65536], P(('row', 'col')), may hold values from 5 to 8, as said below
- send_list: int32 [65536], P(('row', 'col')), may hold values from 0 to 127
- coarse_row: int32 [512], P(('row', 'col')), may hold values from 0 to 127
- coarse_edges: bfloat16 [8192, 512], P(('row', 'col')), may hold values from -6 to 6
- coarse_senders: int32 [8192], P(('row', 'col')), may hold values from 0 to 511
- w_edge: bfloat16 [512, 512], replicated, may hold values from -0.15625 to 0.15625
- w_sender: bfloat16 [512, 512], replicated, may hold values from -0.15625 to 0.15625
- w_receiver: bfloat16 [512, 512], replicated, may hold values from -0.15625 to 0.15625
- w_message: bfloat16 [512, 512], replicated, may hold values from -0.25 to 0.25
- w_node: bfloat16 [512, 512], replicated, may hold values from -0.1875 to 0.1875
- w_gather: bfloat16 [512, 512], replicated, may hold values from -0.1875 to 0.1875
- w_node_out: bfloat16 [512, 512], replicated, may hold values from -0.25 to 0.25
Outputs:
- new_nodes: bfloat16 [65536, 512], P(('row', 'col'))
The draws below stay inside these ranges and needn't reach their ends.
Inputs may be any that keep to these rules, and one draw needn't show every extreme that they name: `fine_senders`: rows below 128 are the partition's own nodes, the next 128 its received rows in direction order, the last 512 the coarse nodes. `degrees`: the first node of every partition uses all 8 slots.
All inputs are finite; a program needn't handle non-finite values.
Results may differ from the reference program's by a relative error of at most 0.0045.
The reference program's roundings to bfloat16 on the way count: a program that leaves them out, or rounds other values in their place, can miss the bound.
Values may be sent and summed in bfloat16 or wider, within the bound.
No kernel may reach another device: no remote copies, remote signals or barrier semaphores. Data moves between devices by JAX's collectives and lax.ppermute only.
A program may use at most 64 MiB of HBM per device.

```python
import jax
import jax.numpy as jnp
from jax import lax

D = 512
NODE_DEV = 128
DEG = 8
SEND = 16
CEDGE_DEV = 16
NODES = 65536
FEDGES = 524288
HALO_ALL = 65536
COARSE = 512
CEDGES = 8192
N_ROW = 32
N_COL = 16


def draw_fine_senders(key, part):
    key = jax.random.fold_in(key, 11)
    keys = jax.random.split(key, 4)
    kinds = jax.random.randint(keys[0], (FEDGES,), 0, 8)
    own_ids = jax.random.randint(keys[1], (FEDGES,), 0, NODE_DEV)
    halo_ids = jax.random.randint(keys[2], (FEDGES,), 0, 8 * SEND) + NODE_DEV
    coarse_ids = jax.random.randint(keys[3], (FEDGES,), 0, COARSE) + NODE_DEV + 8 * SEND
    picked = jnp.where(kinds < 4, own_ids, jnp.where(kinds < 7, halo_ids, coarse_ids))
    return picked.astype(jnp.int32)


def draw_degrees(key, part):
    key = jax.random.fold_in(key, 23)
    counts = jax.random.randint(key, (NODES,), DEG - 3, DEG + 1)
    counts = counts.at[::NODE_DEV].set(DEG)
    return counts.astype(jnp.int32)


def touch_ends(drawn, stream_key, low, top_value):
    index_at = [jax.random.randint(jax.random.fold_in(stream_key, axis), (), 0, length) for axis, length in enumerate(drawn.shape)]
    widest = drawn.shape.index(max(drawn.shape))
    beside = index_at[:widest] + [(index_at[widest] + 1) % drawn.shape[widest]] + index_at[widest + 1:]
    return drawn.at[tuple(index_at)].set(low).at[tuple(beside)].set(top_value)


def block_levels(stream_key, shape, shards, low, top_value):
    level, own = 1.0, jax.random.fold_in(stream_key, 6)
    for axis_at, parts in shards:
        steps = jnp.exp(jax.random.uniform(jax.random.fold_in(own, axis_at), (parts,), jnp.float32, low / len(shards), top_value / len(shards)))
        level = level * jnp.repeat(steps, shape[axis_at] // parts).reshape([-1 if axis == axis_at else 1 for axis in range(len(shape))])
    return level


def gaussian(rng, shape, spread, limit, cuts=(), kind=jnp.bfloat16):
    drawn = jax.random.normal(rng, shape, jnp.float32) * spread
    if len(cuts) > 0:
        drawn = block_levels(rng, shape, cuts, -0.22, 0.18) * drawn
    return jnp.clip(drawn, min=-limit, max=limit).astype(kind)


def setup_inputs(seed: int = 0) -> dict:
    key_list = jax.random.split(jax.random.key(seed), 16)
    node_latents = gaussian(key_list[0], (NODES, D), 1.0, 6.0, ((0, 512),))
    fine_edges = gaussian(key_list[1], (FEDGES, D), 1.0, 6.0, ((0, 512),))
    fine_senders = draw_fine_senders(jax.random.fold_in(key_list[15], 71), 0)
    degrees = draw_degrees(jax.random.fold_in(key_list[15], 71), 0)
    send_list = touch_ends(jax.random.randint(key_list[4], (HALO_ALL,), 0, NODE_DEV), jax.random.fold_in(key_list[4], 1), 0, NODE_DEV - 1).astype(jnp.int32)
    coarse_row = touch_ends(jax.random.randint(key_list[5], (COARSE,), 0, NODE_DEV), jax.random.fold_in(key_list[5], 1), 0, NODE_DEV - 1).astype(jnp.int32)
    coarse_edges = gaussian(key_list[6], (CEDGES, D), 1.0, 6.0, ((0, 512),))
    coarse_senders = touch_ends(jax.random.randint(key_list[7], (CEDGES,), 0, COARSE), jax.random.fold_in(key_list[7], 1), 0, COARSE - 1).astype(jnp.int32)
    w_edge = gaussian(key_list[8], (D, D), (3 * D) ** -0.5, 0.15625)
    w_sender = gaussian(key_list[9], (D, D), (3 * D) ** -0.5, 0.15625)
    w_receiver = gaussian(key_list[10], (D, D), (3 * D) ** -0.5, 0.15625)
    w_message = gaussian(key_list[11], (D, D), D ** -0.5, 0.25)
    w_node = gaussian(key_list[12], (D, D), (2 * D) ** -0.5, 0.1875)
    w_gather = gaussian(key_list[13], (D, D), (2 * D) ** -0.5, 0.1875)
    w_node_out = gaussian(key_list[14], (D, D), D ** -0.5, 0.25)
    return {"node_latents": node_latents, "fine_edges": fine_edges, "fine_senders": fine_senders, "degrees": degrees, "send_list": send_list, "coarse_row": coarse_row, "coarse_edges": coarse_edges, "coarse_senders": coarse_senders, "w_edge": w_edge, "w_sender": w_sender, "w_receiver": w_receiver, "w_message": w_message, "w_node": w_node, "w_gather": w_gather, "w_node_out": w_node_out}


epsilon = 1e-05
DIRECTIONS = ((-1, -1), (-1, 0), (-1, 1), (0, -1), (0, 1), (1, -1), (1, 0), (1, 1))

def layer_norm(values):
    centred = values - lax.optimization_barrier(jnp.mean(values, axis=-1, keepdims=True))
    second = lax.optimization_barrier(jnp.mean(centred * centred, axis=-1, keepdims=True))
    return centred * lax.rsqrt(second + epsilon)

def edge_update(latents, from_sender, from_receiver, w_edge, w_message):
    before = jnp.dot(latents, w_edge, preferred_element_type=jnp.float32) + from_sender + from_receiver
    hidden = jax.nn.silu(before).astype(jnp.bfloat16)
    message = layer_norm(jnp.dot(hidden, w_message, preferred_element_type=jnp.float32))
    return latents.astype(jnp.float32) + message

def reference(node_latents, fine_edges, fine_senders, degrees, send_list, coarse_row, coarse_edges, coarse_senders, w_edge, w_sender, w_receiver, w_message, w_node, w_gather, w_node_out):
    partitions = N_ROW * N_COL
    latent = node_latents.shape[1]
    grid_nodes = node_latents.reshape(N_ROW, N_COL, NODE_DEV, latent)
    send_rows = send_list.reshape(N_ROW, N_COL, 8 * SEND)
    outgoing = jax.vmap(jax.vmap(lambda part_nodes, chosen: jnp.take(part_nodes, chosen, axis=0)))(grid_nodes, send_rows)
    outgoing = outgoing.reshape(N_ROW, N_COL, 8, SEND, latent)
    arrived = []
    for number, offsets in enumerate(DIRECTIONS):
        arrived.append(jnp.roll(outgoing[:, :, 7 - number], (-offsets[0], -offsets[1]), axis=(0, 1)))
    received = jnp.stack(arrived, axis=2).reshape(partitions, 8 * SEND, latent)
    owners = grid_nodes.reshape(partitions, NODE_DEV, latent)
    coarse_table = owners[jnp.arange(partitions), coarse_row]
    coarse_send = jnp.dot(coarse_table, w_sender, preferred_element_type=jnp.float32)
    coarse_recv = jnp.dot(coarse_table, w_receiver, preferred_element_type=jnp.float32)
    coarse_updated = edge_update(coarse_edges, coarse_send[coarse_senders], jnp.repeat(coarse_recv, CEDGE_DEV, axis=0), w_edge, w_message)
    coarse_partial = lax.optimization_barrier(jnp.sum(coarse_updated.reshape(COARSE, CEDGE_DEV, latent), axis=1))

    def partition(inputs):
        own_nodes, halo_nodes, edge_rows, sender_ids, degree_row = inputs
        sender_proj = jnp.concatenate([jnp.dot(own_nodes, w_sender, preferred_element_type=jnp.float32), jnp.dot(halo_nodes, w_sender, preferred_element_type=jnp.float32), coarse_send], axis=0)
        receiver_proj = jnp.dot(own_nodes, w_receiver, preferred_element_type=jnp.float32)
        updated = edge_update(edge_rows, sender_proj[sender_ids], jnp.repeat(receiver_proj, DEG, axis=0), w_edge, w_message)
        updated = updated.reshape(NODE_DEV, DEG, latent)
        in_use = jnp.arange(DEG)[None, :] < degree_row[:, None]
        return lax.optimization_barrier(jnp.sum(jnp.where(in_use[:, :, None], updated, jnp.zeros_like(updated)), axis=1))
    gathered = lax.map(partition, (owners, received, fine_edges.reshape(partitions, NODE_DEV * DEG, latent), fine_senders.reshape(partitions, NODE_DEV * DEG), degrees.reshape(partitions, NODE_DEV)))
    gathered = gathered.at[jnp.arange(partitions), coarse_row].add(coarse_partial)
    summed = gathered.reshape(partitions * NODE_DEV, latent).astype(jnp.bfloat16)
    node_hidden = jax.nn.silu(jnp.dot(node_latents, w_node, preferred_element_type=jnp.float32) + jnp.dot(summed, w_gather, preferred_element_type=jnp.float32)).astype(jnp.bfloat16)
    result = node_latents.astype(jnp.float32) + layer_norm(jnp.dot(node_hidden, w_node_out, preferred_element_type=jnp.float32))
    return result.astype(jnp.bfloat16)
```

```python
import functools

import jax
import jax.numpy as jnp
from jax import lax
from jax.experimental import pallas as pl
from jax.experimental.pallas import tpu as pltpu
from jax.sharding import Mesh
from jax.sharding import PartitionSpec as P

epsilon = 1e-05
AXES = ("y", "zh", "core", "x", "zl")
SIZES = (4, 4, 2, 4, 4)
NEAR = ("zh", "core", "zl")
FAR = ("y", "x")
BF = jnp.bfloat16
F32 = jnp.float32
BLOCK = 256


def dot(a, b):
    return jnp.dot(a, b, preferred_element_type=F32)


def column(row):
    return jnp.transpose(jnp.broadcast_to(row, (128, 128)))


def silu(x):
    half = 0.5 * x
    return half + half * jnp.tanh(half)


def layer_norm(values):
    centred = values - jnp.mean(values, axis=-1, keepdims=True)
    second = jnp.mean(centred * centred, axis=-1, keepdims=True)
    return centred * lax.rsqrt(second + epsilon)


def own_kernel(row_ref, nodes_ref, own_ref, message_ref):
    lanes = lax.broadcasted_iota(jnp.int32, (16, 128), 1)
    chosen = (lanes == row_ref[0]).astype(F32).astype(BF)
    own = dot(chosen, nodes_ref[...])
    own_ref[...] = own.astype(BF)
    rows = jnp.concatenate([own[0:1, 128 * k : 128 * k + 128] for k in range(4)], axis=0)
    message_ref[...] = jnp.broadcast_to(rows.astype(BF)[None], (32, 4, 128))


def pick_kernel(send_ref, nodes_ref, down_ref, up_ref, side_ref):
    lanes = lax.broadcasted_iota(jnp.int32, (128, 128), 1)
    chosen = (column(send_ref[...]) == lanes).astype(F32).astype(BF)
    picked = dot(chosen, nodes_ref[...]).astype(BF)
    up_ref[...] = picked[0:48, :]
    side_ref[...] = picked[48:80, :]
    down_ref[...] = picked[80:128, :]


def onehot(ids, width):
    lanes = lax.broadcasted_iota(jnp.int32, ids.shape, 1)
    parts = [(ids == lanes + 128 * k).astype(F32).astype(BF) for k in range(width // 128)]
    return jnp.concatenate(parts, axis=1)


def place(c):
    return (c & 0x180) | ((c & 0xC) << 3) | ((c & 0x70) >> 2) | (c & 3)


def layer_kernel(row_ref, *refs):
    given, out_ref = refs[:NUM], refs[NUM]
    held, (table, summed_ref, sems) = refs[NUM + 1 : 2 * NUM + 1], refs[2 * NUM + 1 :]
    copies = {}
    for i, name in enumerate(NAMES):
        parts = 4 if name == "edges" else 1
        depth = held[i].shape[0] // parts
        copies[name] = []
        for b in range(parts):
            rows = pl.ds(depth * b, depth)
            sem = sems.at[NUM + b if parts > 1 else i]
            copies[name].append(pltpu.make_async_copy(given[i].at[rows], held[i].at[rows], sem))
    for name in NAMES:
        for copy in copies[name]:
            copy.start()

    def got(name, part=0):
        copies[name][part].wait()
        return held[NAMES.index(name)]

    senders = got("senders")[...]
    csenders = got("csenders")[...]
    degrees = column(got("degrees")[...])
    nodes_ref = got("nodes")
    receiver = dot(nodes_ref[...], got("w_receiver")[...])
    crecv = dot(got("own")[...], held[NAMES.index("w_receiver")][...])
    w_edge = got("w_edge")
    edges = held[NAMES.index("edges")]
    cedges = got("cedges")
    wide = lax.broadcasted_iota(jnp.int32, (32, BLOCK), 1)
    node = lax.broadcasted_iota(jnp.int32, (32, BLOCK), 0)
    spots = jnp.where(senders < 256, -1, place(senders - 256))
    pres, nears, fars, uses, aggs = [], [], [], [], []
    for b in range(4):
        got("edges", b)
        rows = slice(BLOCK * b, BLOCK * b + BLOCK)
        before = dot(edges[rows, :], w_edge[...])
        own = receiver[32 * b : 32 * b + 32, :]
        before = before + jnp.broadcast_to(own[:, None, :], (32, 8, 512)).reshape(BLOCK, 512)
        ids = [column(senders[2 * b + i : 2 * b + i + 1, :]) for i in range(2)]
        nears.append(onehot(jnp.concatenate(ids, axis=0), 256))
        ids = [column(spots[2 * b + i : 2 * b + i + 1, :]) for i in range(2)]
        if b == 3:
            before = jnp.concatenate([before, dot(cedges[...], w_edge[...]) + crecv], axis=0)
            ids.append(column(place(csenders))[:16])
        fars.append(onehot(jnp.concatenate(ids, axis=0), 512))
        pres.append(before)
        deg = degrees[32 * b : 32 * b + 32, :]
        deg = jnp.concatenate([deg, deg], axis=1)
        used = (((wide >> 3) == node) & ((wide & 7) < deg)).astype(F32).astype(BF)
        uses.append(used)
        aggs.append(dot(used, edges[rows, :]))

    table[0:128, :] = nodes_ref[...]
    left, right, above, below = got("left"), got("right"), got("above"), got("below")
    for t, (ref, first) in enumerate(
        ((left, 0), (above, 16), (right, 0), (left, 16), (right, 16), (left, 32), (below, 16), (right, 32))
    ):
        table[128 + 16 * t : 144 + 16 * t, :] = ref[first : first + 16, :]
    coarse = got("coarse")
    w_sender = got("w_sender")
    w_message = got("w_message")
    partial = None
    for b in range(4):
        sender = dot(fars[b], coarse[...])
        near = dot(nears[b], table[...])
        if b == 3:
            near = jnp.concatenate([near, jnp.zeros((16, 512), F32)], axis=0)
        sender = (sender + near).astype(BF)
        before = pres[b] + dot(sender, w_sender[...])
        hidden = silu(before).astype(BF)
        message = layer_norm(dot(hidden, w_message[...]))
        high = message[:BLOCK].astype(BF)
        low = (message[:BLOCK] - high.astype(F32)).astype(BF)
        summed_ref[32 * b : 32 * b + 32, :] = aggs[b] + dot(uses[b], high) + dot(uses[b], low)
        if b == 3:
            updated = cedges[...].astype(F32) + message[BLOCK:]
            partial = jnp.sum(updated, axis=0, keepdims=True)
    node_pre = dot(nodes_ref[...], got("w_node")[...])
    owner = lax.broadcasted_iota(jnp.int32, (128, 1), 0) == row_ref[0]
    summed = summed_ref[...] + jnp.where(owner, partial, jnp.zeros_like(partial))
    hidden = silu(node_pre + dot(summed.astype(BF), got("w_gather")[...])).astype(BF)
    result = nodes_ref[...].astype(F32) + layer_norm(dot(hidden, got("w_node_out")[...]))
    out_ref[...] = result.astype(BF)


NAMES = (
    "senders",
    "csenders",
    "degrees",
    "nodes",
    "w_receiver",
    "own",
    "w_edge",
    "edges",
    "cedges",
    "above",
    "left",
    "right",
    "below",
    "coarse",
    "w_sender",
    "w_message",
    "w_node",
    "w_gather",
    "w_node_out",
)
NUM = len(NAMES)


VMEM = pl.BlockSpec(memory_space=pltpu.VMEM)
SMEM = pl.BlockSpec(memory_space=pltpu.SMEM)
ANY = pl.BlockSpec(memory_space=pl.ANY)


def call(kernel, ins, outs, cost, scratch=(), limit=8):
    return pl.pallas_call(
        kernel,
        in_specs=ins,
        out_specs=[VMEM] * len(outs),
        out_shape=[jax.ShapeDtypeStruct(*o) for o in outs],
        scratch_shapes=scratch,
        cost_estimate=pl.CostEstimate(flops=cost, bytes_accessed=cost // 500, transcendentals=0),
        compiler_params=pltpu.CompilerParams(vmem_limit_bytes=limit * 2**20),
    )


def ring(axis_of, step):
    pairs = []
    for flat in range(512):
        r, c = divmod(flat, 16)
        if axis_of == "row":
            r = (r + step) % 32
        else:
            c = (c + step) % 16
        pairs.append((flat, r * 16 + c))
    return pairs


def body(
    node_latents,
    fine_edges,
    fine_senders,
    degrees,
    send_list,
    coarse_row,
    coarse_edges,
    coarse_senders,
    w_edge,
    w_sender,
    w_receiver,
    w_message,
    w_node,
    w_gather,
    w_node_out,
):
    own, message = call(
        own_kernel, [SMEM, VMEM], [((16, 512), BF), ((32, 4, 128), BF)], 2 * 16 * 128 * 512
    )(coarse_row, node_latents)
    coarse = lax.all_to_all(message, NEAR, 0, 0).reshape(1, 32, 512)
    later, _ = lax.optimization_barrier((send_list, message))
    down, up, side = call(
        pick_kernel,
        [VMEM, VMEM],
        [((48, 512), BF), ((48, 512), BF), ((32, 512), BF)],
        2 * 4000 * 512 * 512,
    )(later.reshape(1, 128), node_latents)
    above = lax.ppermute(down, AXES, ring("row", 1))
    below = lax.ppermute(up, AXES, ring("row", -1))
    coarse = lax.all_to_all(jnp.broadcast_to(coarse, (16, 32, 512)), FAR, 0, 0).reshape(512, 512)
    right = jnp.concatenate([above[32:], side[16:], below[32:]], axis=0)
    left = jnp.concatenate([above[:16], side[:16], below[:16]], axis=0)
    from_left = lax.ppermute(right, AXES, ring("col", 1))
    from_right = lax.ppermute(left, AXES, ring("col", -1))

    csenders = jnp.pad(coarse_senders.reshape(1, 16), ((0, 0), (0, 112)))
    given = dict(
        senders=fine_senders.reshape(8, 128),
        csenders=csenders,
        degrees=degrees.reshape(1, 128),
        nodes=node_latents,
        w_receiver=w_receiver,
        own=own,
        w_edge=w_edge,
        edges=fine_edges,
        cedges=coarse_edges,
        above=above,
        left=from_left,
        right=from_right,
        below=below,
        coarse=coarse,
        w_sender=w_sender,
        w_message=w_message,
        w_node=w_node,
        w_gather=w_gather,
        w_node_out=w_node_out,
    )
    (out,) = call(
        layer_kernel,
        [SMEM] + [ANY] * NUM,
        [((128, 512), BF)],
        2 * 7000 * 512 * 512,
        [pltpu.VMEM(given[name].shape, given[name].dtype) for name in NAMES]
        + [
            pltpu.VMEM((256, 512), BF),
            pltpu.VMEM((128, 512), F32),
            pltpu.SemaphoreType.DMA((NUM + 4,)),
        ],
        limit=56,
    )(coarse_row, *[given[name] for name in NAMES])
    return out


def solution(mesh):
    fine = Mesh(mesh.devices.reshape(SIZES), AXES)
    rows, lists = P(AXES, None), P(AXES)
    placed = (rows, rows, lists, lists, lists, lists, rows, lists) + (P(),) * 7
    return jax.shard_map(body, mesh=fine, in_specs=placed, out_specs=rows, check_vma=False)
```

```python
import functools

import jax
import jax.numpy as jnp
from jax import lax
from jax.experimental import pallas as pl
from jax.experimental.pallas import tpu as pltpu
from jax.sharding import Mesh
from jax.sharding import PartitionSpec as P

epsilon = 1e-05
AXES = ("y", "zh", "core", "x", "zl")
SIZES = (4, 4, 2, 4, 4)
NEAR = ("zh", "core", "zl")
FAR = ("y", "x")
BF = jnp.bfloat16
F32 = jnp.float32
BLOCK = 256


def dot(a, b):
    return jnp.dot(a, b, preferred_element_type=F32)


def column(row):
    return jnp.transpose(jnp.broadcast_to(row, (128, 128)))


def silu(x):
    half = 0.5 * x
    return half + half * jnp.tanh(half)


def layer_norm(values):
    centred = values - jnp.mean(values, axis=-1, keepdims=True)
    second = jnp.mean(centred * centred, axis=-1, keepdims=True)
    return centred * lax.rsqrt(second + epsilon)


def pick_kernel(
    row_ref, odd_ref, send_ref, nodes_ref, first_ref, second_ref, side_ref, own_ref, message_ref
):
    lanes = lax.broadcasted_iota(jnp.int32, (128, 128), 1)
    chosen = (column(send_ref[...]) == lanes).astype(F32).astype(BF)
    picked = dot(chosen, nodes_ref[...])
    odd = odd_ref[0] == 1
    first_ref[...] = jnp.where(odd, picked[0:48, :], picked[80:128, :]).astype(BF)
    second_ref[...] = jnp.where(odd, picked[80:128, :], picked[0:48, :]).astype(BF)
    side_ref[...] = picked[48:80, :].astype(BF)
    chosen = (lanes[:16] == row_ref[0]).astype(F32).astype(BF)
    own = dot(chosen, nodes_ref[...])
    own_ref[...] = own.astype(BF)
    rows = jnp.concatenate([own[0:1, 128 * k : 128 * k + 128] for k in range(4)], axis=0)
    message_ref[...] = jnp.broadcast_to(rows.astype(BF)[None], (32, 4, 128))


def onehot(ids, width):
    lanes = lax.broadcasted_iota(jnp.int32, ids.shape, 1)
    parts = [(ids == lanes + 128 * k).astype(F32).astype(BF) for k in range(width // 128)]
    return jnp.concatenate(parts, axis=1)


def place(c):
    return (c & 0x180) | ((c & 0xC) << 3) | ((c & 0x70) >> 2) | (c & 3)


NAMES = (
    "senders",
    "nodes",
    "w_receiver",
    "w_edge",
    "edges",
    "coarse",
    "degrees",
    "own",
    "cedges",
    "csenders",
    "w_node",
)
NUM = len(NAMES)


def local_kernel(*refs):
    given, held = refs[:NUM], refs[NUM + 6 : 2 * NUM + 6]
    pre_ref, far_ref, near_ref, use_ref, agg_ref, node_pre_ref = refs[NUM : NUM + 6]
    (sems,) = refs[2 * NUM + 6 :]
    copies = {}
    for i, name in enumerate(NAMES):
        parts = 4 if name == "edges" else 1
        depth = held[i].shape[0] // parts
        copies[name] = []
        for b in range(parts):
            rows = pl.ds(depth * b, depth)
            sem = sems.at[NUM + b if parts > 1 else i]
            copies[name].append(pltpu.make_async_copy(given[i].at[rows], held[i].at[rows], sem))
            copies[name][b].start()

    def got(name, part=0):
        copies[name][part].wait()
        return held[NAMES.index(name)]

    senders_ref, nodes_ref = got("senders"), got("nodes")
    w_receiver_ref, w_edge_ref = got("w_receiver"), got("w_edge")
    edges_ref = held[NAMES.index("edges")]
    nodes = nodes_ref[...]
    receiver = dot(nodes, w_receiver_ref[...])
    senders = senders_ref[...]
    spots = jnp.where(senders < 256, -1, place(senders - 256))
    wide = lax.broadcasted_iota(jnp.int32, (32, BLOCK), 1)
    node = lax.broadcasted_iota(jnp.int32, (32, BLOCK), 0)
    for b in range(4):
        rows = slice(BLOCK * b, BLOCK * b + BLOCK)
        got("edges", b)
        before = dot(edges_ref[rows, :], w_edge_ref[...])
        own = receiver[32 * b : 32 * b + 32, :]
        pre_ref[rows, :] = before + jnp.broadcast_to(own[:, None, :], (32, 8, 512)).reshape(BLOCK, 512)
    coarse_ref = got("coarse")
    degrees = column(got("degrees")[...])
    for b in range(4):
        rows = slice(BLOCK * b, BLOCK * b + BLOCK)
        ids = [column(senders[2 * b + i : 2 * b + i + 1, :]) for i in range(2)]
        near_ref[rows, :] = onehot(jnp.concatenate(ids, axis=0), 256)
        ids = [column(spots[2 * b + i : 2 * b + i + 1, :]) for i in range(2)]
        chosen = onehot(jnp.concatenate(ids, axis=0), 512)
        far_ref[rows, :] = dot(chosen, coarse_ref[...]).astype(BF)
        deg = degrees[32 * b : 32 * b + 32, :]
        deg = jnp.concatenate([deg, deg], axis=1)
        used = (((wide >> 3) == node) & ((wide & 7) < deg)).astype(F32).astype(BF)
        use_ref[32 * b : 32 * b + 32, :] = used
        agg_ref[32 * b : 32 * b + 32, :] = dot(used, edges_ref[rows, :])
    own_ref, cedges_ref, csenders_ref = got("own"), got("cedges"), got("csenders")
    coarse = dot(cedges_ref[...], w_edge_ref[...])
    pre_ref[1024:1040, :] = coarse + dot(own_ref[...], w_receiver_ref[...])
    chosen = onehot(column(place(csenders_ref[...]))[:16], 512)
    far_ref[1024:1040, :] = dot(chosen, coarse_ref[...]).astype(BF)
    node_pre_ref[...] = dot(nodes, got("w_node")[...])


def final_kernel(
    row_ref,
    odd_ref,
    pre_ref,
    far_ref,
    near_ref,
    use_ref,
    agg_ref,
    node_pre_ref,
    nodes_ref,
    cedges_ref,
    row_first_ref,
    row_second_ref,
    col_first_ref,
    col_second_ref,
    w_sender_ref,
    w_message_ref,
    w_gather_ref,
    w_node_out_ref,
    out_ref,
    table,
    summed_ref,
):
    def fill(left, right, above, below):
        spots = (
            (left, 0),
            (above, 16),
            (right, 0),
            (left, 16),
            (right, 16),
            (left, 32),
            (below, 16),
            (right, 32),
        )
        for t, (ref, first) in enumerate(spots):
            table[128 + 16 * t : 144 + 16 * t, :] = ref[first : first + 16, :]

    table[0:128, :] = nodes_ref[...]
    for odd_row in range(2):
        for odd_col in range(2):
            above, below = (row_first_ref, row_second_ref) if odd_row else (row_second_ref, row_first_ref)
            left, right = (col_first_ref, col_second_ref) if odd_col else (col_second_ref, col_first_ref)

            @pl.when((odd_ref[0] == odd_row) & (odd_ref[1] == odd_col))
            def _(left=left, right=right, above=above, below=below):
                fill(left, right, above, below)

    partial = None
    for b in range(4):
        rows = slice(BLOCK * b, BLOCK * b + BLOCK)
        sender = dot(near_ref[rows, :], table[...]).astype(BF) + far_ref[rows, :]
        if b == 3:
            rows = slice(BLOCK * b, BLOCK * b + BLOCK + 16)
            sender = jnp.concatenate([sender, far_ref[1024:1040, :]], axis=0)
        before = pre_ref[rows, :] + dot(sender, w_sender_ref[...])
        hidden = silu(before).astype(BF)
        message = layer_norm(dot(hidden, w_message_ref[...]))
        used = use_ref[32 * b : 32 * b + 32, :]
        high = message[:BLOCK].astype(BF)
        low = (message[:BLOCK] - high.astype(F32)).astype(BF)
        summed_ref[32 * b : 32 * b + 32, :] = (
            agg_ref[32 * b : 32 * b + 32, :] + dot(used, high) + dot(used, low)
        )
        if b == 3:
            updated = cedges_ref[...].astype(F32) + message[BLOCK:]
            partial = jnp.sum(updated, axis=0, keepdims=True)
    owner = lax.broadcasted_iota(jnp.int32, (128, 1), 0) == row_ref[0]
    summed = summed_ref[...] + jnp.where(owner, partial, jnp.zeros_like(partial))
    hidden = silu(node_pre_ref[...] + dot(summed.astype(BF), w_gather_ref[...])).astype(BF)
    result = nodes_ref[...].astype(F32) + layer_norm(dot(hidden, w_node_out_ref[...]))
    out_ref[...] = result.astype(BF)


VMEM = pl.BlockSpec(memory_space=pltpu.VMEM)
SMEM = pl.BlockSpec(memory_space=pltpu.SMEM)
HBM = pl.BlockSpec(memory_space=pltpu.HBM)
ANY = pl.BlockSpec(memory_space=pl.ANY)


def call(kernel, ins, outs, cost, scratch=(), limit=8):
    return pl.pallas_call(
        kernel,
        in_specs=ins,
        out_specs=[VMEM] * len(outs),
        out_shape=[jax.ShapeDtypeStruct(*o) for o in outs],
        scratch_shapes=scratch,
        cost_estimate=pl.CostEstimate(flops=cost, bytes_accessed=cost // 500, transcendentals=0),
        compiler_params=pltpu.CompilerParams(vmem_limit_bytes=limit * 2**20),
    )


def swap(axis, odd):
    pairs = []
    for flat in range(512):
        at = list(divmod(flat, 16))
        step = 1 if at[axis] % 2 == odd else -1
        at[axis] = (at[axis] + step) % (32, 16)[axis]
        pairs.append((flat, at[0] * 16 + at[1]))
    return pairs


def body(
    node_latents,
    fine_edges,
    fine_senders,
    degrees,
    send_list,
    coarse_row,
    coarse_edges,
    coarse_senders,
    w_edge,
    w_sender,
    w_receiver,
    w_message,
    w_node,
    w_gather,
    w_node_out,
):
    odd = jnp.stack([lax.axis_index("core"), lax.axis_index("zl") % 2]).astype(jnp.int32)
    first, second, side, own, message = call(
        pick_kernel,
        [SMEM, SMEM, VMEM, VMEM],
        [
            ((48, 512), BF),
            ((48, 512), BF),
            ((32, 512), BF),
            ((16, 512), BF),
            ((32, 4, 128), BF),
        ],
        2 * 144 * 128 * 512,
    )(coarse_row, odd, send_list.reshape(1, 128), node_latents)
    z_rows = lax.all_to_all(message, NEAR, 0, 0)
    row_first = lax.ppermute(first, AXES, swap(0, 0))
    row_second = lax.ppermute(second, AXES, swap(0, 1))
    above = jnp.where(odd[0] == 1, row_first, row_second)
    below = jnp.where(odd[0] == 1, row_second, row_first)
    right = jnp.concatenate([above[32:], side[16:], below[32:]], axis=0)
    left = jnp.concatenate([above[:16], side[:16], below[:16]], axis=0)
    col_first = lax.ppermute(jnp.where(odd[1] == 1, left, right), AXES, swap(1, 0))
    col_second = lax.ppermute(jnp.where(odd[1] == 1, right, left), AXES, swap(1, 1))
    z_rows = z_rows.reshape(1, 32, 512)
    coarse = lax.all_to_all(jnp.broadcast_to(z_rows, (16, 32, 512)), FAR, 0, 0).reshape(512, 512)
    csenders = jnp.pad(coarse_senders.reshape(1, 16), ((0, 0), (0, 112)))
    given = dict(
        senders=fine_senders.reshape(8, 128),
        csenders=csenders,
        degrees=degrees.reshape(1, 128),
        own=own,
        nodes=node_latents,
        edges=fine_edges,
        cedges=coarse_edges,
        coarse=coarse,
        w_edge=w_edge,
        w_receiver=w_receiver,
        w_node=w_node,
    )
    kept = ("coarse", "own", "senders", "csenders", "degrees")
    pre, far, near, use, agg, node_pre = call(
        local_kernel,
        [ANY if name in kept else HBM for name in NAMES],
        [
            ((1040, 512), F32),
            ((1040, 512), BF),
            ((1024, 256), BF),
            ((128, BLOCK), BF),
            ((128, 512), F32),
            ((128, 512), F32),
        ],
        2 * 3500 * 512 * 512,
        [pltpu.VMEM(given[name].shape, given[name].dtype) for name in NAMES]
        + [pltpu.SemaphoreType.DMA((NUM + 4,))],
        limit=12,
    )(*[given[name] for name in NAMES])
    (out,) = call(
        final_kernel,
        [SMEM, SMEM] + [VMEM] * 16,
        [((128, 512), BF)],
        2 * 5000 * 512 * 512,
        [pltpu.VMEM((256, 512), BF), pltpu.VMEM((128, 512), F32)],
    )(
        coarse_row,
        odd,
        pre,
        far,
        near,
        use,
        agg,
        node_pre,
        node_latents,
        coarse_edges,
        row_first,
        row_second,
        col_first,
        col_second,
        w_sender,
        w_message,
        w_gather,
        w_node_out,
    )
    return out


def solution(mesh):
    fine = Mesh(mesh.devices.reshape(SIZES), AXES)
    rows, lists = P(AXES, None), P(AXES)
    placed = (rows, rows, lists, lists, lists, lists, rows, lists) + (P(),) * 7
    return jax.shard_map(body, mesh=fine, in_specs=placed, out_specs=rows, check_vma=False)
```

```python
import functools

import jax
import jax.numpy as jnp
from jax import lax
from jax.experimental import pallas as pl
from jax.experimental.pallas import tpu as pltpu
from jax.sharding import Mesh
from jax.sharding import PartitionSpec as P

epsilon = 1e-05
AXES = ("y", "zh", "core", "x", "zl")
SIZES = (4, 4, 2, 4, 4)
NEAR = ("zh", "core", "zl")
FAR = ("y", "x")
BF = jnp.bfloat16
F32 = jnp.float32
BLOCK = 256


def dot(a, b):
    return jnp.dot(a, b, preferred_element_type=F32)


def column(row):
    return jnp.transpose(jnp.broadcast_to(row, (128, 128)))


def silu(x):
    half = 0.5 * x
    return half + half * jnp.tanh(half)


def layer_norm(values):
    centred = values - jnp.mean(values, axis=-1, keepdims=True)
    second = jnp.mean(centred * centred, axis=-1, keepdims=True)
    return centred * lax.rsqrt(second + epsilon)


def pick_kernel(
    row_ref, send_ref, nodes_ref, first_ref, second_ref, side_ref, own_ref, message_ref
):
    lanes = lax.broadcasted_iota(jnp.int32, (128, 128), 1)
    chosen = (column(send_ref[...]) == lanes).astype(F32).astype(BF)
    picked = dot(chosen, nodes_ref[...])
    odd = lax.axis_index("core") == 1
    first_ref[...] = jnp.where(odd, picked[0:48, :], picked[80:128, :]).astype(BF)
    second_ref[...] = jnp.where(odd, picked[80:128, :], picked[0:48, :]).astype(BF)
    side_ref[...] = picked[48:80, :].astype(BF)
    chosen = (lanes[:16] == row_ref[0]).astype(F32).astype(BF)
    own = dot(chosen, nodes_ref[...])
    own_ref[...] = own.astype(BF)
    rows = jnp.concatenate([own[0:1, 128 * k : 128 * k + 128] for k in range(4)], axis=0)
    message_ref[...] = jnp.broadcast_to(rows.astype(BF)[None], (32, 4, 128))


def onehot(ids, width):
    lanes = lax.broadcasted_iota(jnp.int32, ids.shape, 1)
    parts = [(ids == lanes + 128 * k).astype(F32).astype(BF) for k in range(width // 128)]
    return jnp.concatenate(parts, axis=1)


def place(c):
    return (c & 0x180) | ((c & 0xC) << 3) | ((c & 0x70) >> 2) | (c & 3)


def local_kernel(
    senders_ref,
    csenders_ref,
    degrees_ref,
    own_ref,
    nodes_ref,
    edges_ref,
    cedges_ref,
    coarse_ref,
    w_edge_ref,
    w_receiver_ref,
    pre_ref,
    far_ref,
    near_ref,
    use_ref,
    agg_ref,
):
    nodes = nodes_ref[...]
    receiver = dot(nodes, w_receiver_ref[...])
    senders = senders_ref[...]
    spots = jnp.where(senders < 256, -1, place(senders - 256))
    wide = lax.broadcasted_iota(jnp.int32, (32, BLOCK), 1)
    node = lax.broadcasted_iota(jnp.int32, (32, BLOCK), 0)
    for b in range(4):
        rows = slice(BLOCK * b, BLOCK * b + BLOCK)
        before = dot(edges_ref[rows, :], w_edge_ref[...])
        own = receiver[32 * b : 32 * b + 32, :]
        pre_ref[rows, :] = before + jnp.broadcast_to(own[:, None, :], (32, 8, 512)).reshape(BLOCK, 512)
    degrees = column(degrees_ref[...])
    for b in range(4):
        rows = slice(BLOCK * b, BLOCK * b + BLOCK)
        ids = [column(senders[2 * b + i : 2 * b + i + 1, :]) for i in range(2)]
        near_ref[rows, :] = onehot(jnp.concatenate(ids, axis=0), 256)
        ids = [column(spots[2 * b + i : 2 * b + i + 1, :]) for i in range(2)]
        chosen = onehot(jnp.concatenate(ids, axis=0), 512)
        far_ref[rows, :] = dot(chosen, coarse_ref[...]).astype(BF)
        deg = degrees[32 * b : 32 * b + 32, :]
        deg = jnp.concatenate([deg, deg], axis=1)
        used = (((wide >> 3) == node) & ((wide & 7) < deg)).astype(F32).astype(BF)
        use_ref[32 * b : 32 * b + 32, :] = used
        agg_ref[32 * b : 32 * b + 32, :] = dot(used, edges_ref[rows, :])
    coarse = dot(cedges_ref[...], w_edge_ref[...])
    pre_ref[1024:1040, :] = coarse + dot(own_ref[...], w_receiver_ref[...])
    chosen = onehot(column(place(csenders_ref[...]))[:16], 512)
    far_ref[1024:1040, :] = dot(chosen, coarse_ref[...]).astype(BF)


def final_kernel(
    row_ref,
    pre_ref,
    far_ref,
    near_ref,
    use_ref,
    agg_ref,
    nodes_ref,
    cedges_ref,
    row_first_ref,
    row_second_ref,
    col_first_ref,
    col_second_ref,
    w_sender_ref,
    w_message_ref,
    w_node_ref,
    w_gather_ref,
    w_node_out_ref,
    out_ref,
    table,
    summed_ref,
):
    odd_row = lax.axis_index("core") == 1
    odd_col = lax.axis_index("zl") % 2 == 1
    table[0:128, :] = nodes_ref[...]
    above = jnp.where(odd_row, row_first_ref[...], row_second_ref[...])
    below = jnp.where(odd_row, row_second_ref[...], row_first_ref[...])
    left = jnp.where(odd_col, col_first_ref[...], col_second_ref[...])
    right = jnp.where(odd_col, col_second_ref[...], col_first_ref[...])
    table[128:144, :] = left[0:16]
    table[144:160, :] = above[16:32]
    table[160:176, :] = right[0:16]
    table[176:192, :] = left[16:32]
    table[192:208, :] = right[16:32]
    table[208:224, :] = left[32:48]
    table[224:240, :] = below[16:32]
    table[240:256, :] = right[32:48]
    node_pre = dot(nodes_ref[...], w_node_ref[...])
    partial = None
    for b in range(4):
        rows = slice(BLOCK * b, BLOCK * b + BLOCK)
        sender = dot(near_ref[rows, :], table[...]).astype(BF) + far_ref[rows, :]
        if b == 3:
            rows = slice(BLOCK * b, BLOCK * b + BLOCK + 16)
            sender = jnp.concatenate([sender, far_ref[1024:1040, :]], axis=0)
        before = pre_ref[rows, :] + dot(sender, w_sender_ref[...])
        hidden = silu(before).astype(BF)
        message = layer_norm(dot(hidden, w_message_ref[...]))
        used = use_ref[32 * b : 32 * b + 32, :]
        high = message[:BLOCK].astype(BF)
        low = (message[:BLOCK] - high.astype(F32)).astype(BF)
        summed_ref[32 * b : 32 * b + 32, :] = (
            agg_ref[32 * b : 32 * b + 32, :] + dot(used, high) + dot(used, low)
        )
        if b == 3:
            updated = cedges_ref[...].astype(F32) + message[BLOCK:]
            partial = jnp.sum(updated, axis=0, keepdims=True)
    owner = lax.broadcasted_iota(jnp.int32, (128, 1), 0) == row_ref[0]
    summed = summed_ref[...] + jnp.where(owner, partial, jnp.zeros_like(partial))
    hidden = silu(node_pre + dot(summed.astype(BF), w_gather_ref[...])).astype(BF)
    result = nodes_ref[...].astype(F32) + layer_norm(dot(hidden, w_node_out_ref[...]))
    out_ref[...] = result.astype(BF)


VMEM = pl.BlockSpec(memory_space=pltpu.VMEM)
SMEM = pl.BlockSpec(memory_space=pltpu.SMEM)


def call(kernel, ins, outs, cost, scratch=(), limit=8):
    return pl.pallas_call(
        kernel,
        in_specs=ins,
        out_specs=[VMEM] * len(outs),
        out_shape=[jax.ShapeDtypeStruct(*o) for o in outs],
        scratch_shapes=scratch,
        cost_estimate=pl.CostEstimate(flops=cost, bytes_accessed=cost // 500, transcendentals=0),
        compiler_params=pltpu.CompilerParams(vmem_limit_bytes=limit * 2**20),
    )


def swap(axis, odd):
    pairs = []
    for flat in range(512):
        at = list(divmod(flat, 16))
        step = 1 if at[axis] % 2 == odd else -1
        at[axis] = (at[axis] + step) % (32, 16)[axis]
        pairs.append((flat, at[0] * 16 + at[1]))
    return pairs


def body(
    node_latents,
    fine_edges,
    fine_senders,
    degrees,
    send_list,
    coarse_row,
    coarse_edges,
    coarse_senders,
    w_edge,
    w_sender,
    w_receiver,
    w_message,
    w_node,
    w_gather,
    w_node_out,
):
    odd_row = lax.axis_index("core") == 1
    odd_col = lax.axis_index("zl") % 2 == 1
    first, second, side, own, message = call(
        pick_kernel,
        [SMEM, VMEM, VMEM],
        [
            ((48, 512), BF),
            ((48, 512), BF),
            ((32, 512), BF),
            ((16, 512), BF),
            ((32, 4, 128), BF),
        ],
        2 * 144 * 128 * 512,
    )(coarse_row, send_list.reshape(1, 128), node_latents)
    z_rows = lax.all_to_all(message, NEAR, 0, 0)
    row_first = lax.ppermute(first, AXES, swap(0, 0))
    row_second = lax.ppermute(second, AXES, swap(0, 1))
    above = jnp.where(odd_row, row_first, row_second)
    below = jnp.where(odd_row, row_second, row_first)
    right = jnp.concatenate([above[32:], side[16:], below[32:]], axis=0)
    left = jnp.concatenate([above[:16], side[:16], below[:16]], axis=0)
    col_first = lax.ppermute(jnp.where(odd_col, left, right), AXES, swap(1, 0))
    col_second = lax.ppermute(jnp.where(odd_col, right, left), AXES, swap(1, 1))
    z_rows = z_rows.reshape(1, 32, 512)
    coarse = lax.all_to_all(jnp.broadcast_to(z_rows, (16, 32, 512)), FAR, 0, 0).reshape(512, 512)
    csenders = jnp.pad(coarse_senders.reshape(1, 16), ((0, 0), (0, 112)))
    pre, far, near, use, agg = call(
        local_kernel,
        [VMEM] * 10,
        [
            ((1040, 512), F32),
            ((1040, 512), BF),
            ((1024, 256), BF),
            ((128, BLOCK), BF),
            ((128, 512), F32),
        ],
        2 * 3500 * 512 * 512,
    )(
        fine_senders.reshape(8, 128),
        csenders,
        degrees.reshape(1, 128),
        own,
        node_latents,
        fine_edges,
        coarse_edges,
        coarse,
        w_edge,
        w_receiver,
    )
    (out,) = call(
        final_kernel,
        [SMEM] + [VMEM] * 16,
        [((128, 512), BF)],
        2 * 5000 * 512 * 512,
        [pltpu.VMEM((256, 512), BF), pltpu.VMEM((128, 512), F32)],
    )(
        coarse_row,
        pre,
        far,
        near,
        use,
        agg,
        node_latents,
        coarse_edges,
        row_first,
        row_second,
        col_first,
        col_second,
        w_sender,
        w_message,
        w_node,
        w_gather,
        w_node_out,
    )
    return out


def solution(mesh):
    fine = Mesh(mesh.devices.reshape(SIZES), AXES)
    rows, lists = P(AXES, None), P(AXES)
    placed = (rows, rows, lists, lists, lists, lists, rows, lists) + (P(),) * 7
    return jax.shard_map(body, mesh=fine, in_specs=placed, out_specs=rows, check_vma=False)
```

```python
import functools

import jax
import jax.numpy as jnp
from jax import lax
from jax.experimental import pallas as pl
from jax.experimental.pallas import tpu as pltpu
from jax.sharding import Mesh
from jax.sharding import PartitionSpec as P

epsilon = 1e-05
AXES = ("y", "zh", "core", "x", "zl")
SIZES = (4, 4, 2, 4, 4)
NEAR = ("zh", "core", "zl")
FAR = ("y", "x")
BF = jnp.bfloat16
F32 = jnp.float32
BLOCK = 256


def dot(a, b):
    return jnp.dot(a, b, preferred_element_type=F32)


def column(row):
    return jnp.transpose(jnp.broadcast_to(row, (128, 128)))


def silu(x):
    half = 0.5 * x
    return half + half * jnp.tanh(half)


def layer_norm(values):
    centred = values - jnp.mean(values, axis=-1, keepdims=True)
    second = jnp.mean(centred * centred, axis=-1, keepdims=True)
    return centred * lax.rsqrt(second + epsilon)


def pick_kernel(
    row_from,
    send_from,
    nodes_from,
    first_ref,
    second_ref,
    side_ref,
    own_ref,
    message_ref,
    row_ref,
    send_ref,
    nodes_ref,
    sems,
):
    copies = [
        pltpu.make_async_copy(source, target, sems.at[i])
        for i, (source, target) in enumerate(
            ((nodes_from, nodes_ref), (send_from, send_ref), (row_from, row_ref))
        )
    ]
    for copy in copies:
        copy.start()
    for copy in copies:
        copy.wait()
    lanes = lax.broadcasted_iota(jnp.int32, (128, 128), 1)
    chosen = (column(send_ref[...]) == lanes).astype(F32).astype(BF)
    picked = dot(chosen, nodes_ref[...])
    odd = lax.axis_index("core") == 1
    first_ref[...] = jnp.where(odd, picked[0:48, :], picked[80:128, :]).astype(BF)
    second_ref[...] = jnp.where(odd, picked[80:128, :], picked[0:48, :]).astype(BF)
    side_ref[...] = picked[48:80, :].astype(BF)
    chosen = (lanes[:16] == row_ref[0]).astype(F32).astype(BF)
    own = dot(chosen, nodes_ref[...])
    own_ref[...] = own.astype(BF)
    rows = jnp.concatenate([own[0:1, 128 * k : 128 * k + 128] for k in range(4)], axis=0)
    message_ref[...] = jnp.broadcast_to(rows.astype(BF)[None], (32, 4, 128))


def onehot(ids, width):
    lanes = lax.broadcasted_iota(jnp.int32, ids.shape, 1)
    parts = [(ids == lanes + 128 * k).astype(F32).astype(BF) for k in range(width // 128)]
    return jnp.concatenate(parts, axis=1)


def place(c):
    return (c & 0x180) | ((c & 0xC) << 3) | ((c & 0x70) >> 2) | (c & 3)


def local_kernel(
    senders_ref,
    csenders_ref,
    degrees_ref,
    own_ref,
    nodes_ref,
    edges_ref,
    cedges_ref,
    coarse_ref,
    w_edge_ref,
    w_receiver_ref,
    pre_ref,
    far_ref,
    near_ref,
    use_ref,
    agg_ref,
):
    nodes = nodes_ref[...]
    receiver = dot(nodes, w_receiver_ref[...])
    senders = senders_ref[...]
    spots = jnp.where(senders < 256, -1, place(senders - 256))
    wide = lax.broadcasted_iota(jnp.int32, (32, BLOCK), 1)
    node = lax.broadcasted_iota(jnp.int32, (32, BLOCK), 0)
    for b in range(4):
        rows = slice(BLOCK * b, BLOCK * b + BLOCK)
        before = dot(edges_ref[rows, :], w_edge_ref[...])
        own = receiver[32 * b : 32 * b + 32, :]
        pre_ref[rows, :] = before + jnp.broadcast_to(own[:, None, :], (32, 8, 512)).reshape(BLOCK, 512)
    degrees = column(degrees_ref[...])
    for b in range(4):
        rows = slice(BLOCK * b, BLOCK * b + BLOCK)
        ids = [column(senders[2 * b + i : 2 * b + i + 1, :]) for i in range(2)]
        near_ref[rows, :] = onehot(jnp.concatenate(ids, axis=0), 256)
        ids = [column(spots[2 * b + i : 2 * b + i + 1, :]) for i in range(2)]
        chosen = onehot(jnp.concatenate(ids, axis=0), 512)
        far_ref[rows, :] = dot(chosen, coarse_ref[...]).astype(BF)
        deg = degrees[32 * b : 32 * b + 32, :]
        deg = jnp.concatenate([deg, deg], axis=1)
        used = (((wide >> 3) == node) & ((wide & 7) < deg)).astype(F32).astype(BF)
        use_ref[32 * b : 32 * b + 32, :] = used
        agg_ref[32 * b : 32 * b + 32, :] = dot(used, edges_ref[rows, :])
    coarse = dot(cedges_ref[...], w_edge_ref[...])
    pre_ref[1024:1040, :] = coarse + dot(own_ref[...], w_receiver_ref[...])
    csenders = jnp.concatenate([csenders_ref[...], jnp.zeros((1, 112), jnp.int32)], axis=1)
    chosen = onehot(column(place(csenders))[:16], 512)
    far_ref[1024:1040, :] = dot(chosen, coarse_ref[...]).astype(BF)


def final_kernel(
    row_ref,
    pre_ref,
    far_ref,
    near_ref,
    use_ref,
    agg_ref,
    nodes_ref,
    cedges_ref,
    row_first_ref,
    row_second_ref,
    col_first_ref,
    col_second_ref,
    w_sender_ref,
    w_message_ref,
    w_node_ref,
    w_gather_ref,
    w_node_out_ref,
    out_ref,
    table,
    summed_ref,
):
    odd_row = lax.axis_index("core") == 1
    odd_col = lax.axis_index("zl") % 2 == 1
    table[0:128, :] = nodes_ref[...]
    above = jnp.where(odd_row, row_first_ref[...], row_second_ref[...])
    below = jnp.where(odd_row, row_second_ref[...], row_first_ref[...])
    left = jnp.where(odd_col, col_first_ref[...], col_second_ref[...])
    right = jnp.where(odd_col, col_second_ref[...], col_first_ref[...])
    table[128:144, :] = left[0:16]
    table[144:160, :] = above[16:32]
    table[160:176, :] = right[0:16]
    table[176:192, :] = left[16:32]
    table[192:208, :] = right[16:32]
    table[208:224, :] = left[32:48]
    table[224:240, :] = below[16:32]
    table[240:256, :] = right[32:48]
    node_pre = dot(nodes_ref[...], w_node_ref[...])
    partial = None
    hiddens = []
    for b in range(4):
        rows = slice(BLOCK * b, BLOCK * b + BLOCK)
        sender = dot(near_ref[rows, :], table[...]).astype(BF) + far_ref[rows, :]
        if b == 3:
            rows = slice(BLOCK * b, BLOCK * b + BLOCK + 16)
            sender = jnp.concatenate([sender, far_ref[1024:1040, :]], axis=0)
        before = pre_ref[rows, :] + dot(sender, w_sender_ref[...])
        hiddens.append(silu(before).astype(BF))
    for b in range(4):
        hidden = hiddens[b]
        message = layer_norm(dot(hidden, w_message_ref[...]))
        used = use_ref[32 * b : 32 * b + 32, :]
        high = message[:BLOCK].astype(BF)
        low = (message[:BLOCK] - high.astype(F32)).astype(BF)
        summed_ref[32 * b : 32 * b + 32, :] = (
            agg_ref[32 * b : 32 * b + 32, :] + dot(used, high) + dot(used, low)
        )
        if b == 3:
            updated = cedges_ref[...].astype(F32) + message[BLOCK:]
            partial = jnp.sum(updated, axis=0, keepdims=True)
    owner = lax.broadcasted_iota(jnp.int32, (128, 1), 0) == row_ref[...]
    summed = summed_ref[...] + jnp.where(owner, partial, jnp.zeros_like(partial))
    hidden = silu(node_pre + dot(summed.astype(BF), w_gather_ref[...])).astype(BF)
    result = nodes_ref[...].astype(F32) + layer_norm(dot(hidden, w_node_out_ref[...]))
    out_ref[...] = result.astype(BF)


VMEM = pl.BlockSpec(memory_space=pltpu.VMEM)
ANY = pl.BlockSpec(memory_space=pl.ANY)


def call(kernel, ins, outs, cost, scratch=(), limit=8):
    return pl.pallas_call(
        kernel,
        in_specs=ins,
        out_specs=[VMEM] * len(outs),
        out_shape=[jax.ShapeDtypeStruct(*o) for o in outs],
        scratch_shapes=scratch,
        cost_estimate=pl.CostEstimate(flops=cost, bytes_accessed=cost // 500, transcendentals=0),
        compiler_params=pltpu.CompilerParams(vmem_limit_bytes=limit * 2**20),
    )


def swap(axis, odd):
    pairs = []
    for flat in range(512):
        at = list(divmod(flat, 16))
        step = 1 if at[axis] % 2 == odd else -1
        at[axis] = (at[axis] + step) % (32, 16)[axis]
        pairs.append((flat, at[0] * 16 + at[1]))
    return pairs


def body(
    node_latents,
    fine_edges,
    fine_senders,
    degrees,
    send_list,
    coarse_row,
    coarse_edges,
    coarse_senders,
    w_edge,
    w_sender,
    w_receiver,
    w_message,
    w_node,
    w_gather,
    w_node_out,
):
    odd_row = lax.axis_index("core") == 1
    odd_col = lax.axis_index("zl") % 2 == 1
    first, second, side, own, message = call(
        pick_kernel,
        [ANY] * 3,
        [
            ((48, 512), BF),
            ((48, 512), BF),
            ((32, 512), BF),
            ((16, 512), BF),
            ((32, 4, 128), BF),
        ],
        2 * 144 * 128 * 512,
        [
            pltpu.SMEM((1,), jnp.int32),
            pltpu.VMEM((1, 128), jnp.int32),
            pltpu.VMEM((128, 512), BF),
            pltpu.SemaphoreType.DMA((3,)),
        ],
        limit=56,
    )(coarse_row, send_list.reshape(1, 128), node_latents)
    z_rows = lax.all_to_all(message, NEAR, 0, 0)
    row_first = lax.ppermute(first, AXES, swap(0, 0))
    row_second = lax.ppermute(second, AXES, swap(0, 1))
    above = jnp.where(odd_row, row_first, row_second)
    below = jnp.where(odd_row, row_second, row_first)
    right = jnp.concatenate([above[32:], side[16:], below[32:]], axis=0)
    left = jnp.concatenate([above[:16], side[:16], below[:16]], axis=0)
    col_first = lax.ppermute(jnp.where(odd_col, left, right), AXES, swap(1, 0))
    col_second = lax.ppermute(jnp.where(odd_col, right, left), AXES, swap(1, 1))
    z_rows = z_rows.reshape(1, 32, 512)
    coarse = lax.all_to_all(jnp.broadcast_to(z_rows, (16, 32, 512)), FAR, 0, 0).reshape(512, 512)
    pre, far, near, use, agg = call(
        local_kernel,
        [VMEM] * 10,
        [
            ((1040, 512), F32),
            ((1040, 512), BF),
            ((1024, 256), BF),
            ((128, BLOCK), BF),
            ((128, 512), F32),
        ],
        2 * 3500 * 512 * 512,
    )(
        fine_senders.reshape(8, 128),
        coarse_senders.reshape(1, 16),
        degrees.reshape(1, 128),
        own,
        node_latents,
        fine_edges,
        coarse_edges,
        coarse,
        w_edge,
        w_receiver,
    )
    (out,) = call(
        final_kernel,
        [VMEM] * 17,
        [((128, 512), BF)],
        2 * 5000 * 512 * 512,
        [pltpu.VMEM((256, 512), BF), pltpu.VMEM((128, 512), F32)],
    )(
        coarse_row.reshape(1, 1),
        pre,
        far,
        near,
        use,
        agg,
        node_latents,
        coarse_edges,
        row_first,
        row_second,
        col_first,
        col_second,
        w_sender,
        w_message,
        w_node,
        w_gather,
        w_node_out,
    )
    return out


def solution(mesh):
    fine = Mesh(mesh.devices.reshape(SIZES), AXES)
    rows, lists = P(AXES, None), P(AXES)
    placed = (rows, rows, lists, lists, lists, lists, rows, lists) + (P(),) * 7
    return jax.shard_map(body, mesh=fine, in_specs=placed, out_specs=rows, check_vma=False)
```
